32 devices in a mesh: lat: 4 (over y, x), ma: 8 (over z, core).
Axes of the slice: x: 2, y: 2, z: 4, core: 2. Of those that a mesh axis runs over, the one named last changes fastest.
Arguments:
- fourier: bfloat16 [16, 2, 256, 2560], P(None, None, 'ma', 'lat'), may hold values from -6 to 6
- legendre: bfloat16 [16, 1280, 2, 640], P('ma', 'lat'), may hold values from -0.125 to 0.125
- window: int32 [16], replicated, may hold values from 0 to 639, as said below
- assign: int32 [16], replicated, may hold values from 0 to 15, each once
Outputs:
- coefficients: float32 [16, 2, 640, 256], P('ma', None, 'lat')
The draws below stay inside these ranges and needn't reach their ends.
Inputs may be any that keep to these rules, and one draw needn't show every extreme that they name: `window`: distinct group numbers; 0 and 639 are always among them. `assign`: every position from 0 to 15 appears once.
All inputs are finite; a program needn't handle non-finite values.
Results may differ from the reference program's by a relative error of at most 0.017.
Values may be sent and summed in bfloat16 or wider, within the bound.
A program may use at most 64 MiB of HBM per device.

```python
import jax
import jax.numpy as jnp
from jax import lax

NLAT = 2560
NWAVE = 1280
FIELDS = 256
GROUPS = 16
LATH = 1280
KCOLS = 640
N_LAT = 4


def draw_window(key, part):
    group_count = NWAVE // 2
    inner = jax.random.permutation(key, group_count - 2).astype(jnp.int32) + 1
    ends = jnp.array([0, group_count - 1], dtype=jnp.int32)
    chosen = jnp.concatenate([ends, inner[:GROUPS - 2]])
    shuffle = jax.random.permutation(jax.random.fold_in(key, 7), GROUPS)
    return chosen[shuffle].astype(jnp.int32)


def steps_of(key, dims, split, smallest, top_value):
    gain = 1.0
    for axis_at, parts in split:
        heights = jax.random.uniform(jax.random.fold_in(jax.random.fold_in(key, 6), axis_at), (parts,), jnp.float32, smallest / len(split), top_value / len(split))
        gain = gain * jnp.repeat(jnp.exp(heights), dims[axis_at] // parts).reshape((-1,) + (1,) * (len(dims) - 1 - axis_at))
    return gain


def scatter_about(rng, extent, spread, bound, split=(), kind=jnp.bfloat16):
    result = jax.random.normal(rng, extent, jnp.float32) * spread
    if len(split) > 0:
        result = steps_of(rng, extent, split, -0.22, 0.18) * result
    return jnp.clip(result, min=-bound, max=bound).astype(kind)


def setup_inputs(seed: int = 0) -> dict:
    key_list = jax.random.split(jax.random.key(seed), 5)
    return {
        "fourier": scatter_about(key_list[0], (GROUPS, 2, FIELDS, NLAT), 1.0, 6.0, ((2, 8), (3, 4))),
        "legendre": scatter_about(key_list[1], (GROUPS, LATH, 2, KCOLS), NLAT ** -0.5, 0.125, ((0, 8), (1, 4))),
        "window": draw_window(jax.random.fold_in(key_list[4], 71), 0),
        "assign": jax.random.permutation(key_list[3], GROUPS).astype(jnp.int32),
    }


def pair_source():
    pair_dev = NLAT // (2 * N_LAT)
    hemi_dev = N_LAT // 2
    blocks = jnp.arange(N_LAT, dtype=jnp.int32)
    within = jnp.arange(pair_dev, dtype=jnp.int32)
    starts = 2 * pair_dev * (blocks % hemi_dev) + pair_dev * (blocks // hemi_dev)
    return (starts[:, None] + within[None, :]).reshape(-1).astype(jnp.int32)


def reference(fourier, legendre, window, assign):
    pair_dev = NLAT // (2 * N_LAT)
    half_lat = NLAT // 2
    column_count = NWAVE // 2
    source_rows = pair_source()
    column_base = 2 * jnp.arange(column_count, dtype=jnp.int32)

    def one_group(position):
        slot_index = assign[position]
        stored = lax.dynamic_index_in_dim(fourier, slot_index, 0, keepdims=False)
        latitudes = jnp.transpose(stored, (2, 0, 1)).astype(jnp.float32)
        northern = latitudes[:half_lat]
        southern = latitudes[half_lat:]
        sym_part = (northern + southern).astype(jnp.bfloat16)[source_rows]
        anti_part = (northern - southern).astype(jnp.bfloat16)[source_rows]
        group_id = window[slot_index]
        table_part = lax.dynamic_index_in_dim(legendre, position, 0, keepdims=False)
        results = []
        for parity in range(2):
            column = column_base + parity
            upper_slot = (column >= NWAVE - group_id)[None, :]
            weights = table_part[:, parity, :].astype(jnp.float32)
            lower_table = jnp.where(upper_slot, 0.0, weights).reshape(N_LAT, pair_dev, column_count)
            upper_table = jnp.where(upper_slot, weights, 0.0).reshape(N_LAT, pair_dev, column_count)
            leading = (sym_part if parity == 0 else anti_part)[:, 0, :]
            leading = leading.astype(jnp.float32).reshape(N_LAT, pair_dev, FIELDS)
            trailing = jnp.where((parity + group_id) % 2 == 1, anti_part[:, 1, :], sym_part[:, 1, :])
            trailing = trailing.astype(jnp.float32).reshape(N_LAT, pair_dev, FIELDS)
            partial_value = jnp.einsum("dpk,dpf->dkf", lower_table, leading, precision=lax.Precision.HIGHEST)
            partial_value = partial_value + jnp.einsum("dpk,dpf->dkf", upper_table, trailing, precision=lax.Precision.HIGHEST)
            rounded = lax.optimization_barrier(partial_value.astype(jnp.bfloat16))
            results.append(jnp.sum(rounded.astype(jnp.float32), axis=0))
        return jnp.stack(results, axis=0)

    return lax.map(one_group, jnp.arange(GROUPS, dtype=jnp.int32))
```

```python
import functools

import jax
import jax.numpy as jnp
from jax import lax
from jax.experimental import pallas as pl
from jax.experimental.pallas import tpu as pltpu
from jax.sharding import PartitionSpec as P

MESH = pl.DeviceIdType.MESH
BF16 = jnp.bfloat16
F32 = jnp.float32


def swapped(value, axis, bit):
    mask = 2**bit
    pairs = [(source, source ^ mask) for source in range(lax.axis_size(axis))]
    return lax.ppermute(value, axis, pairs)


def fold_pairs(latitudes, northern):
    pair_rows = latitudes.shape[3] // 2
    leading_rows = latitudes[:, :, :, :pair_rows]
    trailing_rows = latitudes[:, :, :, pair_rows:]
    outgoing = jnp.where(northern, trailing_rows, leading_rows)
    bit_number = lax.axis_size("lat").bit_length() - 2
    arrived = swapped(outgoing, "lat", bit_number)
    staying = jnp.where(northern, leading_rows, trailing_rows)
    upper_rows = jnp.where(northern, staying, arrived).astype(F32)
    lower_rows = jnp.where(northern, arrived, staying).astype(F32)
    return (
        (upper_rows + lower_rows).astype(BF16),
        (upper_rows - lower_rows).astype(BF16),
    )


def plain_on_device(fourier, legendre, window, assign):
    local_groups = legendre.shape[0]
    lat_count = lax.axis_size("lat")
    northern = lax.axis_index("lat") < lat_count // 2
    count = assign.shape[0]
    chosen = assign[:, None] == lax.iota(jnp.int32, count)[None, :]
    ordered = jnp.einsum(
        "iw,wsfr->isfr", chosen.astype(BF16), fourier, preferred_element_type=F32
    ).astype(BF16)
    gathered = lax.all_to_all(ordered, "ma", split_axis=0, concat_axis=2, tiled=True)
    sym_part, anti_part = fold_pairs(gathered, northern)
    all_ids = jnp.sum(jnp.where(chosen, window[None, :], 0), axis=1)
    group_ids = lax.dynamic_slice_in_dim(
        all_ids, lax.axis_index("ma") * local_groups, local_groups
    )
    column_count = legendre.shape[3]
    wave_total = 2 * column_count
    zero_value = jnp.zeros((), BF16)

    def half_term(parity):
        column = 2 * lax.iota(jnp.int32, column_count) + parity
        upper_slot = (column[None, :] >= wave_total - group_ids[:, None])[:, None, :]
        table_part = legendre[:, :, parity, :]
        masked = jnp.stack(
            [
                jnp.where(upper_slot, zero_value, table_part),
                jnp.where(upper_slot, table_part, zero_value),
            ],
            axis=1,
        )
        leading = sym_part[:, 0] if parity == 0 else anti_part[:, 0]
        flipped = ((group_ids + parity) % 2 == 1)[:, None, None]
        trailing = jnp.where(flipped, anti_part[:, 1], sym_part[:, 1])
        sources = jnp.stack([leading, trailing], axis=1)
        return jnp.einsum("gspk,gsfp->gkf", masked, sources, preferred_element_type=F32)

    partials = jnp.stack([half_term(0), half_term(1)], axis=1)
    return lax.psum_scatter(
        partials.astype(BF16), "lat", scatter_dimension=2, tiled=True
    ).astype(F32)


def fused_kernel(
    lat_n,
    ma_n,
    assign_ref,
    window_ref,
    four_ref,
    leg_ref,
    out_ref,
    stage,
    recv,
    weight,
    part,
    landed,
    send_sem,
    recv_sem,
    psend_sem,
    precv_sem,
):
    groups_here = leg_ref.shape[0]
    fields_here = four_ref.shape[2]
    rows = four_ref.shape[3]
    pair = rows // 2
    body = pair // 128 * 128
    tail = pair - body
    kcols = leg_ref.shape[2]
    block = kcols // lat_n
    hemi = lat_n // 2
    half_ma = ma_n // 2
    half_f = half_ma * fields_here

    lat = lax.axis_index("lat")
    ma = lax.axis_index("ma")
    side = lat // hemi
    mine = side
    partner = lax.rem(lat + hemi, lat_n)
    my_half = ma // half_ma

    barrier = pltpu.get_barrier_semaphore()
    met = 0
    for r in range(ma_n):
        there = lax.rem(ma + r, ma_n)
        if r:
            pl.semaphore_signal(barrier, inc=1, device_id=(lat, there), device_id_type=MESH)
            met += 1
        pl.semaphore_signal(barrier, inc=1, device_id=(partner, there), device_id_type=MESH)
        met += 1
    for r in range(1, lat_n):
        if r != hemi:
            pl.semaphore_signal(
                barrier, inc=1, device_id=(lax.rem(lat + r, lat_n), ma), device_id_type=MESH
            )
            met += 1

    def pack(q, g):
        slab = four_ref.at[assign_ref[q * groups_here + g]]
        for t in range(2):
            a = slab[0, :, t * pair : (t + 1) * pair]
            b = slab[1, :, t * pair : (t + 1) * pair]
            stage[g, q, t] = jnp.concatenate(
                [a[:, :body], b[:, :body], a[:, body:], b[:, body:]], axis=1
            )

    def row_copy(g, q, own):
        t = mine if own else 1 - mine
        return pltpu.make_async_remote_copy(
            src_ref=stage.at[g, q, t],
            dst_ref=recv.at[g, side, ma],
            send_sem=send_sem.at[g, q, t],
            recv_sem=recv_sem.at[g, side, ma],
            device_id=(lat if own else partner, q),
            device_id_type=MESH,
        )

    def pack_all(g):
        def step(q, c):
            pack(q, g)
            return c

        lax.fori_loop(0, ma_n, step, 0)

    def send_all(g):
        def step(r, c):
            q = lax.rem(ma + half_ma + r, ma_n)
            row_copy(g, q, False).start()

            @pl.when(q != ma)
            def _():
                row_copy(g, q, True).start()

            return c

        lax.fori_loop(0, ma_n, step, 0)
        pltpu.make_async_copy(
            stage.at[g, ma, mine], recv.at[g, side, ma], recv_sem.at[g, side, ma]
        ).start()

    pack_all(0)
    pl.semaphore_wait(barrier, met)
    send_all(0)
    for g in range(1, groups_here):
        pack_all(g)
        send_all(g)

    ids = [window_ref[assign_ref[ma * groups_here + g]] for g in range(groups_here)]
    for g in range(groups_here):
        for e in range(2):

            def fill(j, c, g=g, e=e):
                start = pl.multiple_of(j * block, 16)
                table = leg_ref[g, e, pl.ds(start, block), :].astype(F32)
                k = start + lax.broadcasted_iota(jnp.int32, (block, 1), 0)
                low = 2 * k + e < 2 * kcols - ids[g]
                lower = jnp.where(low, table, 0.0)
                upper = jnp.where(low, 0.0, table)
                weight[g, e, pl.ds(start, block), :] = jnp.concatenate(
                    [lower[:, :body], upper[:, :body], lower[:, body:], upper[:, body:]],
                    axis=1,
                ).astype(BF16)
                return c

            lax.fori_loop(0, lat_n, fill, 0)

    lane = lax.broadcasted_iota(jnp.int32, (1, rows), 1)
    in_upper = ((lane >= body) & (lane < 2 * body)) | (lane >= 2 * body + tail)

    def part_copy(g, h, r):
        there = lax.rem(lat + r, lat_n)
        return pltpu.make_async_remote_copy(
            src_ref=part.at[g, h, there],
            dst_ref=landed.at[r - 1, g, h],
            send_sem=psend_sem.at[r - 1, g, h],
            recv_sem=precv_sem.at[r - 1, g, h],
            device_id=(there, ma),
            device_id_type=MESH,
        )

    def multiply(g, h):
        def arrive(m, c):
            for ns in range(2):
                piece = recv.at[g, ns, h * half_ma + m]
                pltpu.make_async_copy(piece, piece, recv_sem.at[g, ns, h * half_ma + m]).wait()
            return c

        lax.fori_loop(0, half_ma, arrive, 0)
        north = recv[g, 0, pl.ds(h * half_ma, half_ma)].reshape(half_f, rows).astype(F32)
        south = recv[g, 1, pl.ds(h * half_ma, half_ma)].reshape(half_f, rows).astype(F32)
        for e in range(2):
            odd = lax.rem(ids[g] + e, 2).astype(F32)
            sign = jnp.where(in_upper, 1.0 - 2.0 * odd, 1.0 - 2.0 * e)
            source = (north + sign * south).astype(BF16)
            for d in range(lat_n):
                part[g, h, d, e] = lax.dot_general(
                    weight[g, e, d * block : (d + 1) * block, :],
                    source,
                    (((1,), (1,)), ((), ())),
                    preferred_element_type=F32,
                ).astype(BF16)
        for r in range(1, lat_n):
            part_copy(g, h, r).start()

    def finish(g, h):
        for r in range(1, lat_n):
            part_copy(g, h, r).wait_recv()
        at = pl.multiple_of(h * half_f, 128)
        for e in range(2):
            total = part[g, h, lat, e].astype(F32)
            for r in range(1, lat_n):
                total = total + landed[r - 1, g, h, e].astype(F32)
            out_ref[g, e, :, pl.ds(at, half_f)] = total

    chunks = [(g, (my_half + j) % 2) for g in range(groups_here) for j in range(2)]
    for i, (g, h) in enumerate(chunks):
        multiply(g, h)
        if i:
            finish(*chunks[i - 1])
    finish(*chunks[-1])

    for g in range(groups_here):

        def sent(q, c, g=g):
            row_copy(g, q, False).wait_send()

            @pl.when(q != ma)
            def _():
                row_copy(g, q, True).wait_send()

            return c

        lax.fori_loop(0, ma_n, sent, 0)
    for g, h in chunks:
        for r in range(1, lat_n):
            part_copy(g, h, r).wait_send()


def fused_on_device(fourier, legendre, window, assign):
    lat_n, ma_n = lax.axis_size("lat"), lax.axis_size("ma")
    _, slots, fields_here, rows = fourier.shape
    groups_here, pair, parities, kcols = legendre.shape
    block = kcols // lat_n
    fields = fields_here * ma_n
    tables = jnp.transpose(legendre, (0, 2, 3, 1))
    vmem = pl.BlockSpec(memory_space=pltpu.VMEM)
    smem = pl.BlockSpec(memory_space=pltpu.SMEM)
    dma = pltpu.SemaphoreType.DMA
    return pl.pallas_call(
        functools.partial(fused_kernel, lat_n, ma_n),
        out_shape=jax.ShapeDtypeStruct((groups_here, 2, block, fields), F32),
        in_specs=[smem, smem, vmem, vmem],
        out_specs=vmem,
        scratch_shapes=[
            pltpu.VMEM((groups_here, ma_n, 2, fields_here, rows), BF16),
            pltpu.VMEM((groups_here, 2, ma_n, fields_here, rows), BF16),
            pltpu.VMEM((groups_here, 2, kcols, rows), BF16),
            pltpu.VMEM((groups_here, 2, lat_n, 2, block, fields // 2), BF16),
            pltpu.VMEM((lat_n - 1, groups_here, 2, 2, block, fields // 2), BF16),
            dma((groups_here, ma_n, 2)),
            dma((groups_here, 2, ma_n)),
            dma((lat_n - 1, groups_here, 2)),
            dma((lat_n - 1, groups_here, 2)),
        ],
        compiler_params=pltpu.CompilerParams(
            collective_id=0, has_side_effects=True, vmem_limit_bytes=40 * 2**20
        ),
        cost_estimate=pl.CostEstimate(
            flops=8 * groups_here * kcols * rows * fields,
            bytes_accessed=2 * (fourier.size + legendre.size),
            transcendentals=0,
        ),
    )(assign, window, fourier, tables)


def fits_kernel(mesh, fourier, legendre):
    lat_n, ma_n = mesh.shape["lat"], mesh.shape["ma"]
    fields_here = fourier.shape[2] // ma_n
    pair = legendre.shape[1] // lat_n
    block = legendre.shape[3] // lat_n
    return (
        fourier.shape[1] == 2
        and lat_n == 4
        and ma_n == 8
        and fields_here % 16 == 0
        and (fields_here * ma_n) % 256 == 0
        and (2 * pair) % 128 == 0
        and block % 16 == 0
    )


def solution(mesh):
    def run(fourier, legendre, window, assign):
        fused = fits_kernel(mesh, fourier, legendre)
        return jax.shard_map(
            fused_on_device if fused else plain_on_device,
            mesh=mesh,
            in_specs=(P(None, None, "ma", "lat"), P("ma", "lat", None, None), P(), P()),
            out_specs=P("ma", None, "lat", None),
            check_vma=False,
        )(fourier, legendre, window, assign)

    return run
```

```python
import functools

import jax
import jax.numpy as jnp
from jax import lax
from jax.experimental import pallas as pl
from jax.experimental.pallas import tpu as pltpu
from jax.sharding import PartitionSpec as P

MESH = pl.DeviceIdType.MESH
BF16 = jnp.bfloat16
F32 = jnp.float32


def swapped(value, axis, bit):
    mask = 2**bit
    pairs = [(source, source ^ mask) for source in range(lax.axis_size(axis))]
    return lax.ppermute(value, axis, pairs)


def fold_pairs(latitudes, northern):
    pair_rows = latitudes.shape[3] // 2
    leading_rows = latitudes[:, :, :, :pair_rows]
    trailing_rows = latitudes[:, :, :, pair_rows:]
    outgoing = jnp.where(northern, trailing_rows, leading_rows)
    bit_number = lax.axis_size("lat").bit_length() - 2
    arrived = swapped(outgoing, "lat", bit_number)
    staying = jnp.where(northern, leading_rows, trailing_rows)
    upper_rows = jnp.where(northern, staying, arrived).astype(F32)
    lower_rows = jnp.where(northern, arrived, staying).astype(F32)
    return (
        (upper_rows + lower_rows).astype(BF16),
        (upper_rows - lower_rows).astype(BF16),
    )


def plain_on_device(fourier, legendre, window, assign):
    local_groups = legendre.shape[0]
    lat_count = lax.axis_size("lat")
    northern = lax.axis_index("lat") < lat_count // 2
    count = assign.shape[0]
    chosen = assign[:, None] == lax.iota(jnp.int32, count)[None, :]
    ordered = jnp.einsum(
        "iw,wsfr->isfr", chosen.astype(BF16), fourier, preferred_element_type=F32
    ).astype(BF16)
    gathered = lax.all_to_all(ordered, "ma", split_axis=0, concat_axis=2, tiled=True)
    sym_part, anti_part = fold_pairs(gathered, northern)
    all_ids = jnp.sum(jnp.where(chosen, window[None, :], 0), axis=1)
    group_ids = lax.dynamic_slice_in_dim(
        all_ids, lax.axis_index("ma") * local_groups, local_groups
    )
    column_count = legendre.shape[3]
    wave_total = 2 * column_count
    zero_value = jnp.zeros((), BF16)

    def half_term(parity):
        column = 2 * lax.iota(jnp.int32, column_count) + parity
        upper_slot = (column[None, :] >= wave_total - group_ids[:, None])[:, None, :]
        table_part = legendre[:, :, parity, :]
        masked = jnp.stack(
            [
                jnp.where(upper_slot, zero_value, table_part),
                jnp.where(upper_slot, table_part, zero_value),
            ],
            axis=1,
        )
        leading = sym_part[:, 0] if parity == 0 else anti_part[:, 0]
        flipped = ((group_ids + parity) % 2 == 1)[:, None, None]
        trailing = jnp.where(flipped, anti_part[:, 1], sym_part[:, 1])
        sources = jnp.stack([leading, trailing], axis=1)
        return jnp.einsum("gspk,gsfp->gkf", masked, sources, preferred_element_type=F32)

    partials = jnp.stack([half_term(0), half_term(1)], axis=1)
    return lax.psum_scatter(
        partials.astype(BF16), "lat", scatter_dimension=2, tiled=True
    ).astype(F32)


def fused_kernel(
    lat_n,
    ma_n,
    assign_ref,
    window_ref,
    four_ref,
    leg_ref,
    out_ref,
    stage,
    recv,
    weight,
    part,
    landed,
    send_sem,
    recv_sem,
    psend_sem,
    precv_sem,
):
    groups_here = leg_ref.shape[0]
    fields_here = four_ref.shape[2]
    rows = four_ref.shape[3]
    pair = rows // 2
    body = pair // 128 * 128
    tail = pair - body
    kcols = leg_ref.shape[3]
    block = kcols // lat_n
    hemi = lat_n // 2
    half_ma = ma_n // 2
    half_f = half_ma * fields_here

    lat = lax.axis_index("lat")
    ma = lax.axis_index("ma")
    side = lat // hemi
    mine = side
    partner = lax.rem(lat + hemi, lat_n)
    my_half = ma // half_ma

    barrier = pltpu.get_barrier_semaphore()
    met = 0
    for r in range(ma_n):
        there = lax.rem(ma + r, ma_n)
        if r:
            pl.semaphore_signal(barrier, inc=1, device_id=(lat, there), device_id_type=MESH)
            met += 1
        pl.semaphore_signal(barrier, inc=1, device_id=(partner, there), device_id_type=MESH)
        met += 1
    for r in range(1, lat_n):
        if r != hemi:
            pl.semaphore_signal(
                barrier, inc=1, device_id=(lax.rem(lat + r, lat_n), ma), device_id_type=MESH
            )
            met += 1

    def pack(q, g):
        slab = four_ref.at[assign_ref[q * groups_here + g]]
        for t in range(2):
            a = slab[0, :, t * pair : (t + 1) * pair]
            b = slab[1, :, t * pair : (t + 1) * pair]
            stage[g, q, t] = jnp.concatenate(
                [a[:, :body], b[:, :body], a[:, body:], b[:, body:]], axis=1
            )

    def row_copy(g, q, own):
        t = mine if own else 1 - mine
        return pltpu.make_async_remote_copy(
            src_ref=stage.at[g, q, t],
            dst_ref=recv.at[g, side, ma],
            send_sem=send_sem.at[g, q, t],
            recv_sem=recv_sem.at[g, side, ma],
            device_id=(lat if own else partner, q),
            device_id_type=MESH,
        )

    def pack_all(g):
        def step(q, c):
            pack(q, g)
            return c

        lax.fori_loop(0, ma_n, step, 0)

    def send_all(g):
        def step(r, c):
            q = lax.rem(ma + half_ma + r, ma_n)
            row_copy(g, q, False).start()

            @pl.when(q != ma)
            def _():
                row_copy(g, q, True).start()

            return c

        lax.fori_loop(0, ma_n, step, 0)
        pltpu.make_async_copy(
            stage.at[g, ma, mine], recv.at[g, side, ma], recv_sem.at[g, side, ma]
        ).start()

    pack_all(0)
    pl.semaphore_wait(barrier, met)
    send_all(0)
    for g in range(1, groups_here):
        pack_all(g)
        send_all(g)

    ids = [window_ref[assign_ref[ma * groups_here + g]] for g in range(groups_here)]
    for g in range(groups_here):
        for e in range(2):

            def fill(j, c, g=g, e=e):
                start = pl.multiple_of(j * 128, 128)
                table = leg_ref[g, :, e, pl.ds(start, 128)].astype(F32).T
                k = start + lax.broadcasted_iota(jnp.int32, (128, 1), 0)
                low = 2 * k + e < 2 * kcols - ids[g]
                lower = jnp.where(low, table, 0.0)
                upper = jnp.where(low, 0.0, table)
                weight[g, e, pl.ds(start, 128), :] = jnp.concatenate(
                    [lower[:, :body], upper[:, :body], lower[:, body:], upper[:, body:]],
                    axis=1,
                ).astype(BF16)
                return c

            lax.fori_loop(0, kcols // 128, fill, 0)

    lane = lax.broadcasted_iota(jnp.int32, (1, rows), 1)
    in_upper = ((lane >= body) & (lane < 2 * body)) | (lane >= 2 * body + tail)

    def part_copy(g, h, r):
        there = lax.rem(lat + r, lat_n)
        return pltpu.make_async_remote_copy(
            src_ref=part.at[g, h, there],
            dst_ref=landed.at[r - 1, g, h],
            send_sem=psend_sem.at[r - 1, g, h],
            recv_sem=precv_sem.at[r - 1, g, h],
            device_id=(there, ma),
            device_id_type=MESH,
        )

    def multiply(g, h):
        def arrive(m, c):
            for ns in range(2):
                piece = recv.at[g, ns, h * half_ma + m]
                pltpu.make_async_copy(piece, piece, recv_sem.at[g, ns, h * half_ma + m]).wait()
            return c

        lax.fori_loop(0, half_ma, arrive, 0)
        north = recv[g, 0, pl.ds(h * half_ma, half_ma)].reshape(half_f, rows).astype(F32)
        south = recv[g, 1, pl.ds(h * half_ma, half_ma)].reshape(half_f, rows).astype(F32)
        for e in range(2):
            odd = lax.rem(ids[g] + e, 2).astype(F32)
            sign = jnp.where(in_upper, 1.0 - 2.0 * odd, 1.0 - 2.0 * e)
            source = (north + sign * south).astype(BF16)
            for d in range(lat_n):
                part[g, h, d, e] = lax.dot_general(
                    weight[g, e, d * block : (d + 1) * block, :],
                    source,
                    (((1,), (1,)), ((), ())),
                    preferred_element_type=F32,
                ).astype(BF16)
        for r in range(1, lat_n):
            part_copy(g, h, r).start()

    def finish(g, h):
        for r in range(1, lat_n):
            part_copy(g, h, r).wait_recv()
        at = pl.multiple_of(h * half_f, 128)
        for e in range(2):
            total = part[g, h, lat, e].astype(F32)
            for r in range(1, lat_n):
                total = total + landed[r - 1, g, h, e].astype(F32)
            out_ref[g, e, :, pl.ds(at, half_f)] = total

    chunks = [(g, (my_half + j) % 2) for g in range(groups_here) for j in range(2)]
    for i, (g, h) in enumerate(chunks):
        multiply(g, h)
        if i:
            finish(*chunks[i - 1])
    finish(*chunks[-1])

    for g in range(groups_here):

        def sent(q, c, g=g):
            row_copy(g, q, False).wait_send()

            @pl.when(q != ma)
            def _():
                row_copy(g, q, True).wait_send()

            return c

        lax.fori_loop(0, ma_n, sent, 0)
    for g, h in chunks:
        for r in range(1, lat_n):
            part_copy(g, h, r).wait_send()


def fused_on_device(fourier, legendre, window, assign):
    lat_n, ma_n = lax.axis_size("lat"), lax.axis_size("ma")
    _, slots, fields_here, rows = fourier.shape
    groups_here, pair, parities, kcols = legendre.shape
    block = kcols // lat_n
    fields = fields_here * ma_n
    vmem = pl.BlockSpec(memory_space=pltpu.VMEM)
    smem = pl.BlockSpec(memory_space=pltpu.SMEM)
    dma = pltpu.SemaphoreType.DMA
    return pl.pallas_call(
        functools.partial(fused_kernel, lat_n, ma_n),
        out_shape=jax.ShapeDtypeStruct((groups_here, 2, block, fields), F32),
        in_specs=[smem, smem, vmem, vmem],
        out_specs=vmem,
        scratch_shapes=[
            pltpu.VMEM((groups_here, ma_n, 2, fields_here, rows), BF16),
            pltpu.VMEM((groups_here, 2, ma_n, fields_here, rows), BF16),
            pltpu.VMEM((groups_here, 2, kcols, rows), BF16),
            pltpu.VMEM((groups_here, 2, lat_n, 2, block, fields // 2), BF16),
            pltpu.VMEM((lat_n - 1, groups_here, 2, 2, block, fields // 2), BF16),
            dma((groups_here, ma_n, 2)),
            dma((groups_here, 2, ma_n)),
            dma((lat_n - 1, groups_here, 2)),
            dma((lat_n - 1, groups_here, 2)),
        ],
        compiler_params=pltpu.CompilerParams(
            collective_id=0, has_side_effects=True, vmem_limit_bytes=40 * 2**20
        ),
        cost_estimate=pl.CostEstimate(
            flops=8 * groups_here * kcols * rows * fields,
            bytes_accessed=2 * (fourier.size + legendre.size),
            transcendentals=0,
        ),
    )(assign, window, fourier, legendre)


def fits_kernel(mesh, fourier, legendre):
    lat_n, ma_n = mesh.shape["lat"], mesh.shape["ma"]
    fields_here = fourier.shape[2] // ma_n
    pair = legendre.shape[1] // lat_n
    block = legendre.shape[3] // lat_n
    return (
        fourier.shape[1] == 2
        and lat_n == 4
        and ma_n == 8
        and fields_here % 16 == 0
        and (fields_here * ma_n) % 256 == 0
        and (2 * pair) % 128 == 0
        and block % 16 == 0
        and legendre.shape[3] % 128 == 0
    )


def solution(mesh):
    def run(fourier, legendre, window, assign):
        fused = fits_kernel(mesh, fourier, legendre)
        return jax.shard_map(
            fused_on_device if fused else plain_on_device,
            mesh=mesh,
            in_specs=(P(None, None, "ma", "lat"), P("ma", "lat", None, None), P(), P()),
            out_specs=P("ma", None, "lat", None),
            check_vma=False,
        )(fourier, legendre, window, assign)

    return run
```

```python
import functools

import jax
import jax.numpy as jnp
from jax import lax
from jax.experimental import pallas as pl
from jax.experimental.pallas import tpu as pltpu
from jax.sharding import PartitionSpec as P

MESH = pl.DeviceIdType.MESH
BF16 = jnp.bfloat16
F32 = jnp.float32


def swapped(value, axis, bit):
    mask = 2**bit
    pairs = [(source, source ^ mask) for source in range(lax.axis_size(axis))]
    return lax.ppermute(value, axis, pairs)


def fold_pairs(latitudes, northern):
    pair_rows = latitudes.shape[3] // 2
    leading_rows = latitudes[:, :, :, :pair_rows]
    trailing_rows = latitudes[:, :, :, pair_rows:]
    outgoing = jnp.where(northern, trailing_rows, leading_rows)
    bit_number = lax.axis_size("lat").bit_length() - 2
    arrived = swapped(outgoing, "lat", bit_number)
    staying = jnp.where(northern, leading_rows, trailing_rows)
    upper_rows = jnp.where(northern, staying, arrived).astype(F32)
    lower_rows = jnp.where(northern, arrived, staying).astype(F32)
    return (
        (upper_rows + lower_rows).astype(BF16),
        (upper_rows - lower_rows).astype(BF16),
    )


def plain_on_device(fourier, legendre, window, assign):
    local_groups = legendre.shape[0]
    lat_count = lax.axis_size("lat")
    northern = lax.axis_index("lat") < lat_count // 2
    count = assign.shape[0]
    chosen = assign[:, None] == lax.iota(jnp.int32, count)[None, :]
    ordered = jnp.einsum(
        "iw,wsfr->isfr", chosen.astype(BF16), fourier, preferred_element_type=F32
    ).astype(BF16)
    gathered = lax.all_to_all(ordered, "ma", split_axis=0, concat_axis=2, tiled=True)
    sym_part, anti_part = fold_pairs(gathered, northern)
    all_ids = jnp.sum(jnp.where(chosen, window[None, :], 0), axis=1)
    group_ids = lax.dynamic_slice_in_dim(
        all_ids, lax.axis_index("ma") * local_groups, local_groups
    )
    column_count = legendre.shape[3]
    wave_total = 2 * column_count
    zero_value = jnp.zeros((), BF16)

    def half_term(parity):
        column = 2 * lax.iota(jnp.int32, column_count) + parity
        upper_slot = (column[None, :] >= wave_total - group_ids[:, None])[:, None, :]
        table_part = legendre[:, :, parity, :]
        masked = jnp.stack(
            [
                jnp.where(upper_slot, zero_value, table_part),
                jnp.where(upper_slot, table_part, zero_value),
            ],
            axis=1,
        )
        leading = sym_part[:, 0] if parity == 0 else anti_part[:, 0]
        flipped = ((group_ids + parity) % 2 == 1)[:, None, None]
        trailing = jnp.where(flipped, anti_part[:, 1], sym_part[:, 1])
        sources = jnp.stack([leading, trailing], axis=1)
        return jnp.einsum("gspk,gsfp->gkf", masked, sources, preferred_element_type=F32)

    partials = jnp.stack([half_term(0), half_term(1)], axis=1)
    return lax.psum_scatter(
        partials.astype(BF16), "lat", scatter_dimension=2, tiled=True
    ).astype(F32)


def fused_kernel(
    lat_n,
    ma_n,
    assign_ref,
    window_ref,
    four_hbm,
    leg_hbm,
    out_ref,
    four_ref,
    leg_ref,
    stage,
    recv,
    weight,
    part,
    landed,
    send_sem,
    recv_sem,
    psend_sem,
    precv_sem,
    leg_sem,
    four_sem,
):
    groups_here = leg_ref.shape[0]
    fields_here = four_ref.shape[2]
    rows = four_ref.shape[3]
    pair = rows // 2
    body = pair // 128 * 128
    tail = pair - body
    kcols = leg_ref.shape[3]
    block = kcols // lat_n
    hemi = lat_n // 2
    half_ma = ma_n // 2
    half_f = half_ma * fields_here

    lat = lax.axis_index("lat")
    ma = lax.axis_index("ma")
    side = lat // hemi
    mine = side
    partner = lax.rem(lat + hemi, lat_n)
    my_half = ma // half_ma

    rows_copy = pltpu.make_async_copy(four_hbm, four_ref, four_sem)
    rows_copy.start()
    table_copy = pltpu.make_async_copy(leg_hbm, leg_ref, leg_sem)
    table_copy.start()

    barrier = pltpu.get_barrier_semaphore()
    met = 0
    for r in range(ma_n):
        there = lax.rem(ma + r, ma_n)
        if r:
            pl.semaphore_signal(barrier, inc=1, device_id=(lat, there), device_id_type=MESH)
            met += 1
        pl.semaphore_signal(barrier, inc=1, device_id=(partner, there), device_id_type=MESH)
        met += 1
    for r in range(1, lat_n):
        if r != hemi:
            pl.semaphore_signal(
                barrier, inc=1, device_id=(lax.rem(lat + r, lat_n), ma), device_id_type=MESH
            )
            met += 1

    def pack(q, g):
        slab = four_ref.at[assign_ref[q * groups_here + g]]
        for t in range(2):
            a = slab[0, :, t * pair : (t + 1) * pair]
            b = slab[1, :, t * pair : (t + 1) * pair]
            stage[g, q, t] = jnp.concatenate(
                [a[:, :body], b[:, :body], a[:, body:], b[:, body:]], axis=1
            )

    def row_copy(g, q, own):
        t = mine if own else 1 - mine
        return pltpu.make_async_remote_copy(
            src_ref=stage.at[g, q, t],
            dst_ref=recv.at[g, side, ma],
            send_sem=send_sem.at[g, q, t],
            recv_sem=recv_sem.at[g, side, ma],
            device_id=(lat if own else partner, q),
            device_id_type=MESH,
        )

    def pack_send(g):
        def step(r, c):
            hop = r // 2
            half = lax.rem(my_half + 1 + r, 2)
            q = half * half_ma + lax.rem(ma + hop, half_ma)
            pack(q, g)
            row_copy(g, q, False).start()

            @pl.when(q != ma)
            def _():
                row_copy(g, q, True).start()

            return c

        lax.fori_loop(0, ma_n, step, 0)
        pltpu.make_async_copy(
            stage.at[g, ma, mine], recv.at[g, side, ma], recv_sem.at[g, side, ma]
        ).start()

    rows_copy.wait()
    pl.semaphore_wait(barrier, met)
    for g in range(groups_here):
        pack_send(g)
    table_copy.wait()

    ids = [window_ref[assign_ref[ma * groups_here + g]] for g in range(groups_here)]
    for g in range(groups_here):
        for e in range(2):

            def fill(j, c, g=g, e=e):
                start = pl.multiple_of(j * 128, 128)
                table = leg_ref[g, :, e, pl.ds(start, 128)].astype(F32).T
                k = start + lax.broadcasted_iota(jnp.int32, (128, 1), 0)
                low = 2 * k + e < 2 * kcols - ids[g]
                lower = jnp.where(low, table, 0.0)
                upper = jnp.where(low, 0.0, table)
                weight[g, e, pl.ds(start, 128), :] = jnp.concatenate(
                    [lower[:, :body], upper[:, :body], lower[:, body:], upper[:, body:]],
                    axis=1,
                ).astype(BF16)
                return c

            lax.fori_loop(0, kcols // 128, fill, 0)

    lane = lax.broadcasted_iota(jnp.int32, (1, rows), 1)
    in_upper = ((lane >= body) & (lane < 2 * body)) | (lane >= 2 * body + tail)

    def part_copy(g, h, r):
        there = lax.rem(lat + r, lat_n)
        return pltpu.make_async_remote_copy(
            src_ref=part.at[g, h, there],
            dst_ref=landed.at[r - 1, g, h],
            send_sem=psend_sem.at[r - 1, g, h],
            recv_sem=precv_sem.at[r - 1, g, h],
            device_id=(there, ma),
            device_id_type=MESH,
        )

    def multiply(g, h):
        def arrive(m, c):
            for ns in range(2):
                piece = recv.at[g, ns, h * half_ma + m]
                pltpu.make_async_copy(piece, piece, recv_sem.at[g, ns, h * half_ma + m]).wait()
            return c

        lax.fori_loop(0, half_ma, arrive, 0)
        north = recv[g, 0, pl.ds(h * half_ma, half_ma)].reshape(half_f, rows).astype(F32)
        south = recv[g, 1, pl.ds(h * half_ma, half_ma)].reshape(half_f, rows).astype(F32)
        for e in range(2):
            odd = lax.rem(ids[g] + e, 2).astype(F32)
            sign = jnp.where(in_upper, 1.0 - 2.0 * odd, 1.0 - 2.0 * e)
            source = (north + sign * south).astype(BF16)
            for d in range(lat_n):
                part[g, h, d, e] = lax.dot_general(
                    weight[g, e, d * block : (d + 1) * block, :],
                    source,
                    (((1,), (1,)), ((), ())),
                    preferred_element_type=F32,
                ).astype(BF16)
        for r in range(1, lat_n):
            part_copy(g, h, r).start()

    def finish(g, h):
        for r in range(1, lat_n):
            part_copy(g, h, r).wait_recv()
        at = pl.multiple_of(h * half_f, 128)
        for e in range(2):
            total = part[g, h, lat, e].astype(F32)
            for r in range(1, lat_n):
                total = total + landed[r - 1, g, h, e].astype(F32)
            out_ref[g, e, :, pl.ds(at, half_f)] = total

    chunks = [(g, (my_half + j) % 2) for g in range(groups_here) for j in range(2)]
    for i, (g, h) in enumerate(chunks):
        multiply(g, h)
        if i:
            finish(*chunks[i - 1])
    finish(*chunks[-1])

    for g in range(groups_here):

        def sent(q, c, g=g):
            row_copy(g, q, False).wait_send()

            @pl.when(q != ma)
            def _():
                row_copy(g, q, True).wait_send()

            return c

        lax.fori_loop(0, ma_n, sent, 0)
    for g, h in chunks:
        for r in range(1, lat_n):
            part_copy(g, h, r).wait_send()


def fused_on_device(fourier, legendre, window, assign):
    lat_n, ma_n = lax.axis_size("lat"), lax.axis_size("ma")
    _, slots, fields_here, rows = fourier.shape
    groups_here, pair, parities, kcols = legendre.shape
    block = kcols // lat_n
    fields = fields_here * ma_n
    vmem = pl.BlockSpec(memory_space=pltpu.VMEM)
    smem = pl.BlockSpec(memory_space=pltpu.SMEM)
    hbm = pl.BlockSpec(memory_space=pltpu.HBM)
    dma = pltpu.SemaphoreType.DMA
    return pl.pallas_call(
        functools.partial(fused_kernel, lat_n, ma_n),
        out_shape=jax.ShapeDtypeStruct((groups_here, 2, block, fields), F32),
        in_specs=[smem, smem, hbm, hbm],
        out_specs=vmem,
        scratch_shapes=[
            pltpu.VMEM(fourier.shape, BF16),
            pltpu.VMEM(legendre.shape, BF16),
            pltpu.VMEM((groups_here, ma_n, 2, fields_here, rows), BF16),
            pltpu.VMEM((groups_here, 2, ma_n, fields_here, rows), BF16),
            pltpu.VMEM((groups_here, 2, kcols, rows), BF16),
            pltpu.VMEM((groups_here, 2, lat_n, 2, block, fields // 2), BF16),
            pltpu.VMEM((lat_n - 1, groups_here, 2, 2, block, fields // 2), BF16),
            dma((groups_here, ma_n, 2)),
            dma((groups_here, 2, ma_n)),
            dma((lat_n - 1, groups_here, 2)),
            dma((lat_n - 1, groups_here, 2)),
            dma,
            dma,
        ],
        compiler_params=pltpu.CompilerParams(
            collective_id=0, has_side_effects=True, vmem_limit_bytes=63 * 2**20
        ),
        cost_estimate=pl.CostEstimate(
            flops=8 * groups_here * kcols * rows * fields,
            bytes_accessed=2 * (fourier.size + legendre.size),
            transcendentals=0,
        ),
    )(assign, window, fourier, legendre)


def fits_kernel(mesh, fourier, legendre):
    lat_n, ma_n = mesh.shape["lat"], mesh.shape["ma"]
    fields_here = fourier.shape[2] // ma_n
    pair = legendre.shape[1] // lat_n
    block = legendre.shape[3] // lat_n
    return (
        fourier.shape[1] == 2
        and lat_n == 4
        and ma_n == 8
        and fields_here % 16 == 0
        and (fields_here * ma_n) % 256 == 0
        and (2 * pair) % 128 == 0
        and block % 16 == 0
        and legendre.shape[3] % 128 == 0
    )


def solution(mesh):
    def run(fourier, legendre, window, assign):
        fused = fits_kernel(mesh, fourier, legendre)
        return jax.shard_map(
            fused_on_device if fused else plain_on_device,
            mesh=mesh,
            in_specs=(P(None, None, "ma", "lat"), P("ma", "lat", None, None), P(), P()),
            out_specs=P("ma", None, "lat", None),
            check_vma=False,
        )(fourier, legendre, window, assign)

    return run
```

```python
import functools

import jax
import jax.numpy as jnp
from jax import lax
from jax.experimental import pallas as pl
from jax.experimental.pallas import tpu as pltpu
from jax.sharding import PartitionSpec as P

MESH = pl.DeviceIdType.MESH
BF16 = jnp.bfloat16
F32 = jnp.float32


def swapped(value, axis, bit):
    mask = 2**bit
    pairs = [(source, source ^ mask) for source in range(lax.axis_size(axis))]
    return lax.ppermute(value, axis, pairs)


def fold_pairs(latitudes, northern):
    pair_rows = latitudes.shape[3] // 2
    leading_rows = latitudes[:, :, :, :pair_rows]
    trailing_rows = latitudes[:, :, :, pair_rows:]
    outgoing = jnp.where(northern, trailing_rows, leading_rows)
    bit_number = lax.axis_size("lat").bit_length() - 2
    arrived = swapped(outgoing, "lat", bit_number)
    staying = jnp.where(northern, leading_rows, trailing_rows)
    upper_rows = jnp.where(northern, staying, arrived).astype(F32)
    lower_rows = jnp.where(northern, arrived, staying).astype(F32)
    return (
        (upper_rows + lower_rows).astype(BF16),
        (upper_rows - lower_rows).astype(BF16),
    )


def plain_on_device(fourier, legendre, window, assign):
    local_groups = legendre.shape[0]
    lat_count = lax.axis_size("lat")
    northern = lax.axis_index("lat") < lat_count // 2
    count = assign.shape[0]
    chosen = assign[:, None] == lax.iota(jnp.int32, count)[None, :]
    ordered = jnp.einsum(
        "iw,wsfr->isfr", chosen.astype(BF16), fourier, preferred_element_type=F32
    ).astype(BF16)
    gathered = lax.all_to_all(ordered, "ma", split_axis=0, concat_axis=2, tiled=True)
    sym_part, anti_part = fold_pairs(gathered, northern)
    all_ids = jnp.sum(jnp.where(chosen, window[None, :], 0), axis=1)
    group_ids = lax.dynamic_slice_in_dim(
        all_ids, lax.axis_index("ma") * local_groups, local_groups
    )
    column_count = legendre.shape[3]
    wave_total = 2 * column_count
    zero_value = jnp.zeros((), BF16)

    def half_term(parity):
        column = 2 * lax.iota(jnp.int32, column_count) + parity
        upper_slot = (column[None, :] >= wave_total - group_ids[:, None])[:, None, :]
        table_part = legendre[:, :, parity, :]
        masked = jnp.stack(
            [
                jnp.where(upper_slot, zero_value, table_part),
                jnp.where(upper_slot, table_part, zero_value),
            ],
            axis=1,
        )
        leading = sym_part[:, 0] if parity == 0 else anti_part[:, 0]
        flipped = ((group_ids + parity) % 2 == 1)[:, None, None]
        trailing = jnp.where(flipped, anti_part[:, 1], sym_part[:, 1])
        sources = jnp.stack([leading, trailing], axis=1)
        return jnp.einsum("gspk,gsfp->gkf", masked, sources, preferred_element_type=F32)

    partials = jnp.stack([half_term(0), half_term(1)], axis=1)
    return lax.psum_scatter(
        partials.astype(BF16), "lat", scatter_dimension=2, tiled=True
    ).astype(F32)


def fused_kernel(
    lat_n,
    ma_n,
    assign_ref,
    window_ref,
    four_hbm,
    leg_hbm,
    out_ref,
    four_ref,
    leg_ref,
    stage,
    recv,
    weight,
    part,
    landed,
    send_sem,
    recv_sem,
    psend_sem,
    precv_sem,
    leg_sem,
    four_sem,
):
    groups_here = leg_ref.shape[0]
    fields_here = four_ref.shape[2]
    rows = four_ref.shape[3]
    pair = rows // 2
    body = pair // 128 * 128
    tail = pair - body
    kcols = leg_ref.shape[3]
    block = kcols // lat_n
    hemi = lat_n // 2
    half_ma = ma_n // 2
    half_f = half_ma * fields_here

    lat = lax.axis_index("lat")
    ma = lax.axis_index("ma")
    side = lat // hemi
    mine = side
    partner = lax.rem(lat + hemi, lat_n)
    my_half = ma // half_ma

    rows_copy = pltpu.make_async_copy(four_hbm, four_ref, four_sem)
    rows_copy.start()
    table_copy = pltpu.make_async_copy(leg_hbm, leg_ref, leg_sem)
    table_copy.start()

    barrier = pltpu.get_barrier_semaphore()
    met = 0
    for r in range(ma_n):
        there = lax.rem(ma + r, ma_n)
        if r:
            pl.semaphore_signal(barrier, inc=1, device_id=(lat, there), device_id_type=MESH)
            met += 1
        pl.semaphore_signal(barrier, inc=1, device_id=(partner, there), device_id_type=MESH)
        met += 1
    for r in range(1, lat_n):
        if r != hemi:
            pl.semaphore_signal(
                barrier, inc=1, device_id=(lax.rem(lat + r, lat_n), ma), device_id_type=MESH
            )
            met += 1

    def pack(q, g):
        slab = four_ref.at[assign_ref[q * groups_here + g]]
        for t in range(2):
            a = slab[0, :, t * pair : (t + 1) * pair]
            b = slab[1, :, t * pair : (t + 1) * pair]
            stage[g, q, t] = jnp.concatenate(
                [a[:, :body], b[:, :body], a[:, body:], b[:, body:]], axis=1
            )

    def row_copy(g, q, own):
        t = mine if own else 1 - mine
        return pltpu.make_async_remote_copy(
            src_ref=stage.at[g, q, t],
            dst_ref=recv.at[g, side, ma],
            send_sem=send_sem.at[g, q, t],
            recv_sem=recv_sem.at[g, side, ma],
            device_id=(lat if own else partner, q),
            device_id_type=MESH,
        )

    def pack_send(g):
        def step(r, c):
            hop = lax.rem(r, half_ma)
            half = lax.rem(my_half + 1 + r // half_ma, 2)
            q = half * half_ma + lax.rem(ma + hop, half_ma)
            pack(q, g)
            row_copy(g, q, False).start()

            @pl.when(q != ma)
            def _():
                row_copy(g, q, True).start()

            return c

        lax.fori_loop(0, ma_n, step, 0)
        pltpu.make_async_copy(
            stage.at[g, ma, mine], recv.at[g, side, ma], recv_sem.at[g, side, ma]
        ).start()

    rows_copy.wait()
    pl.semaphore_wait(barrier, met)
    for g in range(groups_here):
        pack_send(g)
    table_copy.wait()

    ids = [window_ref[assign_ref[ma * groups_here + g]] for g in range(groups_here)]
    for g in range(groups_here):
        for e in range(2):

            def fill(j, c, g=g, e=e):
                start = pl.multiple_of(j * 128, 128)
                table = leg_ref[g, :, e, pl.ds(start, 128)].astype(F32).T
                k = start + lax.broadcasted_iota(jnp.int32, (128, 1), 0)
                low = 2 * k + e < 2 * kcols - ids[g]
                lower = jnp.where(low, table, 0.0)
                upper = jnp.where(low, 0.0, table)
                weight[g, e, pl.ds(start, 128), :] = jnp.concatenate(
                    [lower[:, :body], upper[:, :body], lower[:, body:], upper[:, body:]],
                    axis=1,
                ).astype(BF16)
                return c

            lax.fori_loop(0, kcols // 128, fill, 0)

    lane = lax.broadcasted_iota(jnp.int32, (1, rows), 1)
    in_upper = ((lane >= body) & (lane < 2 * body)) | (lane >= 2 * body + tail)

    def part_copy(g, h, r):
        there = lax.rem(lat + r, lat_n)
        return pltpu.make_async_remote_copy(
            src_ref=part.at[g, h, there],
            dst_ref=landed.at[r - 1, g, h],
            send_sem=psend_sem.at[r - 1, g, h],
            recv_sem=precv_sem.at[r - 1, g, h],
            device_id=(there, ma),
            device_id_type=MESH,
        )

    def multiply(g, h):
        def arrive(m, c):
            for ns in range(2):
                piece = recv.at[g, ns, h * half_ma + m]
                pltpu.make_async_copy(piece, piece, recv_sem.at[g, ns, h * half_ma + m]).wait()
            return c

        lax.fori_loop(0, half_ma, arrive, 0)
        north = recv[g, 0, pl.ds(h * half_ma, half_ma)].reshape(half_f, rows).astype(F32)
        south = recv[g, 1, pl.ds(h * half_ma, half_ma)].reshape(half_f, rows).astype(F32)
        for e in range(2):
            odd = lax.rem(ids[g] + e, 2).astype(F32)
            sign = jnp.where(in_upper, 1.0 - 2.0 * odd, 1.0 - 2.0 * e)
            source = (north + sign * south).astype(BF16)
            for d in range(lat_n):
                part[g, h, d, e] = lax.dot_general(
                    weight[g, e, d * block : (d + 1) * block, :],
                    source,
                    (((1,), (1,)), ((), ())),
                    preferred_element_type=F32,
                ).astype(BF16)
        for r in range(1, lat_n):
            part_copy(g, h, r).start()

    def finish(g, h):
        for r in range(1, lat_n):
            part_copy(g, h, r).wait_recv()
        at = pl.multiple_of(h * half_f, 128)
        for e in range(2):
            total = part[g, h, lat, e].astype(F32)
            for r in range(1, lat_n):
                total = total + landed[r - 1, g, h, e].astype(F32)
            out_ref[g, e, :, pl.ds(at, half_f)] = total

    chunks = [(g, (my_half + 1 + j) % 2) for g in range(groups_here) for j in range(2)]
    for i, (g, h) in enumerate(chunks):
        multiply(g, h)
        if i:
            finish(*chunks[i - 1])
    finish(*chunks[-1])

    for g in range(groups_here):

        def sent(q, c, g=g):
            row_copy(g, q, False).wait_send()

            @pl.when(q != ma)
            def _():
                row_copy(g, q, True).wait_send()

            return c

        lax.fori_loop(0, ma_n, sent, 0)
    for g, h in chunks:
        for r in range(1, lat_n):
            part_copy(g, h, r).wait_send()


def fused_on_device(fourier, legendre, window, assign):
    lat_n, ma_n = lax.axis_size("lat"), lax.axis_size("ma")
    _, slots, fields_here, rows = fourier.shape
    groups_here, pair, parities, kcols = legendre.shape
    block = kcols // lat_n
    fields = fields_here * ma_n
    vmem = pl.BlockSpec(memory_space=pltpu.VMEM)
    smem = pl.BlockSpec(memory_space=pltpu.SMEM)
    hbm = pl.BlockSpec(memory_space=pltpu.HBM)
    dma = pltpu.SemaphoreType.DMA
    return pl.pallas_call(
        functools.partial(fused_kernel, lat_n, ma_n),
        out_shape=jax.ShapeDtypeStruct((groups_here, 2, block, fields), F32),
        in_specs=[smem, smem, hbm, hbm],
        out_specs=vmem,
        scratch_shapes=[
            pltpu.VMEM(fourier.shape, BF16),
            pltpu.VMEM(legendre.shape, BF16),
            pltpu.VMEM((groups_here, ma_n, 2, fields_here, rows), BF16),
            pltpu.VMEM((groups_here, 2, ma_n, fields_here, rows), BF16),
            pltpu.VMEM((groups_here, 2, kcols, rows), BF16),
            pltpu.VMEM((groups_here, 2, lat_n, 2, block, fields // 2), BF16),
            pltpu.VMEM((lat_n - 1, groups_here, 2, 2, block, fields // 2), BF16),
            dma((groups_here, ma_n, 2)),
            dma((groups_here, 2, ma_n)),
            dma((lat_n - 1, groups_here, 2)),
            dma((lat_n - 1, groups_here, 2)),
            dma,
            dma,
        ],
        compiler_params=pltpu.CompilerParams(
            collective_id=0, has_side_effects=True, vmem_limit_bytes=63 * 2**20
        ),
        cost_estimate=pl.CostEstimate(
            flops=8 * groups_here * kcols * rows * fields,
            bytes_accessed=2 * (fourier.size + legendre.size),
            transcendentals=0,
        ),
    )(assign, window, fourier, legendre)


def fits_kernel(mesh, fourier, legendre):
    lat_n, ma_n = mesh.shape["lat"], mesh.shape["ma"]
    fields_here = fourier.shape[2] // ma_n
    pair = legendre.shape[1] // lat_n
    block = legendre.shape[3] // lat_n
    return (
        fourier.shape[1] == 2
        and lat_n == 4
        and ma_n == 8
        and fields_here % 16 == 0
        and (fields_here * ma_n) % 256 == 0
        and (2 * pair) % 128 == 0
        and block % 16 == 0
        and legendre.shape[3] % 128 == 0
    )


def solution(mesh):
    def run(fourier, legendre, window, assign):
        fused = fits_kernel(mesh, fourier, legendre)
        return jax.shard_map(
            fused_on_device if fused else plain_on_device,
            mesh=mesh,
            in_specs=(P(None, None, "ma", "lat"), P("ma", "lat", None, None), P(), P()),
            out_specs=P("ma", None, "lat", None),
            check_vma=False,
        )(fourier, legendre, window, assign)

    return run
```

```python
import functools

import jax
import jax.numpy as jnp
from jax import lax
from jax.experimental import pallas as pl
from jax.experimental.pallas import tpu as pltpu
from jax.sharding import PartitionSpec as P

MESH = pl.DeviceIdType.MESH
BF16 = jnp.bfloat16
F32 = jnp.float32


def swapped(value, axis, bit):
    mask = 2**bit
    pairs = [(source, source ^ mask) for source in range(lax.axis_size(axis))]
    return lax.ppermute(value, axis, pairs)


def fold_pairs(latitudes, northern):
    pair_rows = latitudes.shape[3] // 2
    leading_rows = latitudes[:, :, :, :pair_rows]
    trailing_rows = latitudes[:, :, :, pair_rows:]
    outgoing = jnp.where(northern, trailing_rows, leading_rows)
    bit_number = lax.axis_size("lat").bit_length() - 2
    arrived = swapped(outgoing, "lat", bit_number)
    staying = jnp.where(northern, leading_rows, trailing_rows)
    upper_rows = jnp.where(northern, staying, arrived).astype(F32)
    lower_rows = jnp.where(northern, arrived, staying).astype(F32)
    return (
        (upper_rows + lower_rows).astype(BF16),
        (upper_rows - lower_rows).astype(BF16),
    )


def plain_on_device(fourier, legendre, window, assign):
    local_groups = legendre.shape[0]
    lat_count = lax.axis_size("lat")
    northern = lax.axis_index("lat") < lat_count // 2
    count = assign.shape[0]
    chosen = assign[:, None] == lax.iota(jnp.int32, count)[None, :]
    ordered = jnp.einsum(
        "iw,wsfr->isfr", chosen.astype(BF16), fourier, preferred_element_type=F32
    ).astype(BF16)
    gathered = lax.all_to_all(ordered, "ma", split_axis=0, concat_axis=2, tiled=True)
    sym_part, anti_part = fold_pairs(gathered, northern)
    all_ids = jnp.sum(jnp.where(chosen, window[None, :], 0), axis=1)
    group_ids = lax.dynamic_slice_in_dim(
        all_ids, lax.axis_index("ma") * local_groups, local_groups
    )
    column_count = legendre.shape[3]
    wave_total = 2 * column_count
    zero_value = jnp.zeros((), BF16)

    def half_term(parity):
        column = 2 * lax.iota(jnp.int32, column_count) + parity
        upper_slot = (column[None, :] >= wave_total - group_ids[:, None])[:, None, :]
        table_part = legendre[:, :, parity, :]
        masked = jnp.stack(
            [
                jnp.where(upper_slot, zero_value, table_part),
                jnp.where(upper_slot, table_part, zero_value),
            ],
            axis=1,
        )
        leading = sym_part[:, 0] if parity == 0 else anti_part[:, 0]
        flipped = ((group_ids + parity) % 2 == 1)[:, None, None]
        trailing = jnp.where(flipped, anti_part[:, 1], sym_part[:, 1])
        sources = jnp.stack([leading, trailing], axis=1)
        return jnp.einsum("gspk,gsfp->gkf", masked, sources, preferred_element_type=F32)

    partials = jnp.stack([half_term(0), half_term(1)], axis=1)
    return lax.psum_scatter(
        partials.astype(BF16), "lat", scatter_dimension=2, tiled=True
    ).astype(F32)


def fused_kernel(
    lat_n,
    ma_n,
    assign_ref,
    window_ref,
    four_hbm,
    leg_hbm,
    out_hbm,
    out_ref,
    four_ref,
    leg_ref,
    stage,
    recv,
    weight,
    part,
    landed,
    send_sem,
    recv_sem,
    psend_sem,
    precv_sem,
    leg_sem,
    four_sem,
    out_sem,
):
    groups_here = leg_ref.shape[0]
    fields_here = four_ref.shape[2]
    rows = four_ref.shape[3]
    pair = rows // 2
    body = pair // 128 * 128
    tail = pair - body
    kcols = leg_ref.shape[3]
    block = kcols // lat_n
    hemi = lat_n // 2
    half_ma = ma_n // 2
    half_f = half_ma * fields_here

    lat = lax.axis_index("lat")
    ma = lax.axis_index("ma")
    side = lat // hemi
    mine = side
    partner = lax.rem(lat + hemi, lat_n)
    my_half = ma // half_ma

    rows_copy = pltpu.make_async_copy(four_hbm, four_ref, four_sem)
    rows_copy.start()
    table_copy = pltpu.make_async_copy(leg_hbm, leg_ref, leg_sem)
    table_copy.start()

    barrier = pltpu.get_barrier_semaphore()
    met = 0
    for r in range(ma_n):
        there = lax.rem(ma + r, ma_n)
        if r:
            pl.semaphore_signal(barrier, inc=1, device_id=(lat, there), device_id_type=MESH)
            met += 1
        pl.semaphore_signal(barrier, inc=1, device_id=(partner, there), device_id_type=MESH)
        met += 1
    for r in range(1, lat_n):
        if r != hemi:
            pl.semaphore_signal(
                barrier, inc=1, device_id=(lax.rem(lat + r, lat_n), ma), device_id_type=MESH
            )
            met += 1

    def pack(q, g):
        slab = four_ref.at[assign_ref[q * groups_here + g]]
        for t in range(2):
            a = slab[0, :, t * pair : (t + 1) * pair]
            b = slab[1, :, t * pair : (t + 1) * pair]
            stage[g, q, t] = jnp.concatenate(
                [a[:, :body], b[:, :body], a[:, body:], b[:, body:]], axis=1
            )

    def row_copy(g, q, own):
        t = mine if own else 1 - mine
        return pltpu.make_async_remote_copy(
            src_ref=stage.at[g, q, t],
            dst_ref=recv.at[g, side, ma],
            send_sem=send_sem.at[g, q, t],
            recv_sem=recv_sem.at[g, side, ma],
            device_id=(lat if own else partner, q),
            device_id_type=MESH,
        )

    def pack_send(g):
        def step(r, c):
            hop = r // 2
            half = lax.rem(my_half + 1 + r, 2)
            q = half * half_ma + lax.rem(ma + hop, half_ma)
            pack(q, g)
            row_copy(g, q, False).start()

            @pl.when(q != ma)
            def _():
                row_copy(g, q, True).start()

            return c

        lax.fori_loop(0, ma_n, step, 0)
        pltpu.make_async_copy(
            stage.at[g, ma, mine], recv.at[g, side, ma], recv_sem.at[g, side, ma]
        ).start()

    rows_copy.wait()
    pl.semaphore_wait(barrier, met)
    for g in range(groups_here):
        pack_send(g)
    table_copy.wait()

    ids = [window_ref[assign_ref[ma * groups_here + g]] for g in range(groups_here)]
    for g in range(groups_here):
        for e in range(2):

            def fill(j, c, g=g, e=e):
                start = pl.multiple_of(j * 128, 128)
                table = leg_ref[g, :, e, pl.ds(start, 128)].astype(F32).T
                k = start + lax.broadcasted_iota(jnp.int32, (128, 1), 0)
                low = 2 * k + e < 2 * kcols - ids[g]
                lower = jnp.where(low, table, 0.0)
                upper = jnp.where(low, 0.0, table)
                weight[g, e, pl.ds(start, 128), :] = jnp.concatenate(
                    [lower[:, :body], upper[:, :body], lower[:, body:], upper[:, body:]],
                    axis=1,
                ).astype(BF16)
                return c

            lax.fori_loop(0, kcols // 128, fill, 0)

    lane = lax.broadcasted_iota(jnp.int32, (1, rows), 1)
    in_upper = ((lane >= body) & (lane < 2 * body)) | (lane >= 2 * body + tail)

    def part_copy(g, h, e, r):
        there = lax.rem(lat + r, lat_n)
        return pltpu.make_async_remote_copy(
            src_ref=part.at[g, h, there, e],
            dst_ref=landed.at[r - 1, g, h, e],
            send_sem=psend_sem.at[r - 1, g, h, e],
            recv_sem=precv_sem.at[r - 1, g, h, e],
            device_id=(there, ma),
            device_id_type=MESH,
        )

    def multiply(g, h):
        def arrive(m, c):
            for ns in range(2):
                piece = recv.at[g, ns, h * half_ma + m]
                pltpu.make_async_copy(piece, piece, recv_sem.at[g, ns, h * half_ma + m]).wait()
            return c

        lax.fori_loop(0, half_ma, arrive, 0)
        north = recv[g, 0, pl.ds(h * half_ma, half_ma)].reshape(half_f, rows).astype(F32)
        south = recv[g, 1, pl.ds(h * half_ma, half_ma)].reshape(half_f, rows).astype(F32)
        for e in range(2):
            odd = lax.rem(ids[g] + e, 2).astype(F32)
            sign = jnp.where(in_upper, 1.0 - 2.0 * odd, 1.0 - 2.0 * e)
            source = (north + sign * south).astype(BF16)
            for d in range(lat_n):
                part[g, h, d, e] = lax.dot_general(
                    weight[g, e, d * block : (d + 1) * block, :],
                    source,
                    (((1,), (1,)), ((), ())),
                    preferred_element_type=F32,
                ).astype(BF16)
            for r in range(1, lat_n):
                part_copy(g, h, e, r).start()

    def out_copy(g, h, e):
        at = pl.multiple_of(h * half_f, 128)
        return pltpu.make_async_copy(
            out_ref.at[g, e, h], out_hbm.at[g, e, :, pl.ds(at, half_f)], out_sem.at[g, e, h]
        )

    def finish(g, h):
        for e in range(2):
            for r in range(1, lat_n):
                part_copy(g, h, e, r).wait_recv()
            total = part[g, h, lat, e].astype(F32)
            for r in range(1, lat_n):
                total = total + landed[r - 1, g, h, e].astype(F32)
            out_ref[g, e, h] = total
            out_copy(g, h, e).start()

    chunks = [(g, (my_half + j) % 2) for g in range(groups_here) for j in range(2)]
    for i, (g, h) in enumerate(chunks):
        multiply(g, h)
        if i:
            finish(*chunks[i - 1])
    finish(*chunks[-1])

    for g in range(groups_here):

        def sent(q, c, g=g):
            row_copy(g, q, False).wait_send()

            @pl.when(q != ma)
            def _():
                row_copy(g, q, True).wait_send()

            return c

        lax.fori_loop(0, ma_n, sent, 0)
    for g, h in chunks:
        for e in range(2):
            for r in range(1, lat_n):
                part_copy(g, h, e, r).wait_send()
            out_copy(g, h, e).wait()


def fused_on_device(fourier, legendre, window, assign):
    lat_n, ma_n = lax.axis_size("lat"), lax.axis_size("ma")
    _, slots, fields_here, rows = fourier.shape
    groups_here, pair, parities, kcols = legendre.shape
    block = kcols // lat_n
    fields = fields_here * ma_n
    smem = pl.BlockSpec(memory_space=pltpu.SMEM)
    hbm = pl.BlockSpec(memory_space=pltpu.HBM)
    dma = pltpu.SemaphoreType.DMA
    return pl.pallas_call(
        functools.partial(fused_kernel, lat_n, ma_n),
        out_shape=jax.ShapeDtypeStruct((groups_here, 2, block, fields), F32),
        in_specs=[smem, smem, hbm, hbm],
        out_specs=hbm,
        scratch_shapes=[
            pltpu.VMEM((groups_here, 2, 2, block, fields // 2), F32),
            pltpu.VMEM(fourier.shape, BF16),
            pltpu.VMEM(legendre.shape, BF16),
            pltpu.VMEM((groups_here, ma_n, 2, fields_here, rows), BF16),
            pltpu.VMEM((groups_here, 2, ma_n, fields_here, rows), BF16),
            pltpu.VMEM((groups_here, 2, kcols, rows), BF16),
            pltpu.VMEM((groups_here, 2, lat_n, 2, block, fields // 2), BF16),
            pltpu.VMEM((lat_n - 1, groups_here, 2, 2, block, fields // 2), BF16),
            dma((groups_here, ma_n, 2)),
            dma((groups_here, 2, ma_n)),
            dma((lat_n - 1, groups_here, 2, 2)),
            dma((lat_n - 1, groups_here, 2, 2)),
            dma,
            dma,
            dma((groups_here, 2, 2)),
        ],
        compiler_params=pltpu.CompilerParams(
            collective_id=0, has_side_effects=True, vmem_limit_bytes=63 * 2**20
        ),
        cost_estimate=pl.CostEstimate(
            flops=8 * groups_here * kcols * rows * fields,
            bytes_accessed=2 * (fourier.size + legendre.size),
            transcendentals=0,
        ),
    )(assign, window, fourier, legendre)


def fits_kernel(mesh, fourier, legendre):
    lat_n, ma_n = mesh.shape["lat"], mesh.shape["ma"]
    fields_here = fourier.shape[2] // ma_n
    pair = legendre.shape[1] // lat_n
    block = legendre.shape[3] // lat_n
    return (
        fourier.shape[1] == 2
        and lat_n == 4
        and ma_n == 8
        and fields_here % 16 == 0
        and (fields_here * ma_n) % 256 == 0
        and (2 * pair) % 128 == 0
        and block % 16 == 0
        and legendre.shape[3] % 128 == 0
    )


def solution(mesh):
    def run(fourier, legendre, window, assign):
        fused = fits_kernel(mesh, fourier, legendre)
        return jax.shard_map(
            fused_on_device if fused else plain_on_device,
            mesh=mesh,
            in_specs=(P(None, None, "ma", "lat"), P("ma", "lat", None, None), P(), P()),
            out_specs=P("ma", None, "lat", None),
            check_vma=False,
        )(fourier, legendre, window, assign)

    return run
```

```python
import functools

import jax
import jax.numpy as jnp
from jax import lax
from jax.experimental import pallas as pl
from jax.experimental.pallas import tpu as pltpu
from jax.sharding import PartitionSpec as P

MESH = pl.DeviceIdType.MESH
BF16 = jnp.bfloat16
F32 = jnp.float32


def swapped(value, axis, bit):
    mask = 2**bit
    pairs = [(source, source ^ mask) for source in range(lax.axis_size(axis))]
    return lax.ppermute(value, axis, pairs)


def fold_pairs(latitudes, northern):
    pair_rows = latitudes.shape[3] // 2
    leading_rows = latitudes[:, :, :, :pair_rows]
    trailing_rows = latitudes[:, :, :, pair_rows:]
    outgoing = jnp.where(northern, trailing_rows, leading_rows)
    bit_number = lax.axis_size("lat").bit_length() - 2
    arrived = swapped(outgoing, "lat", bit_number)
    staying = jnp.where(northern, leading_rows, trailing_rows)
    upper_rows = jnp.where(northern, staying, arrived).astype(F32)
    lower_rows = jnp.where(northern, arrived, staying).astype(F32)
    return (
        (upper_rows + lower_rows).astype(BF16),
        (upper_rows - lower_rows).astype(BF16),
    )


def plain_on_device(fourier, legendre, window, assign):
    local_groups = legendre.shape[0]
    lat_count = lax.axis_size("lat")
    northern = lax.axis_index("lat") < lat_count // 2
    count = assign.shape[0]
    chosen = assign[:, None] == lax.iota(jnp.int32, count)[None, :]
    ordered = jnp.einsum(
        "iw,wsfr->isfr", chosen.astype(BF16), fourier, preferred_element_type=F32
    ).astype(BF16)
    gathered = lax.all_to_all(ordered, "ma", split_axis=0, concat_axis=2, tiled=True)
    sym_part, anti_part = fold_pairs(gathered, northern)
    all_ids = jnp.sum(jnp.where(chosen, window[None, :], 0), axis=1)
    group_ids = lax.dynamic_slice_in_dim(
        all_ids, lax.axis_index("ma") * local_groups, local_groups
    )
    column_count = legendre.shape[3]
    wave_total = 2 * column_count
    zero_value = jnp.zeros((), BF16)

    def half_term(parity):
        column = 2 * lax.iota(jnp.int32, column_count) + parity
        upper_slot = (column[None, :] >= wave_total - group_ids[:, None])[:, None, :]
        table_part = legendre[:, :, parity, :]
        masked = jnp.stack(
            [
                jnp.where(upper_slot, zero_value, table_part),
                jnp.where(upper_slot, table_part, zero_value),
            ],
            axis=1,
        )
        leading = sym_part[:, 0] if parity == 0 else anti_part[:, 0]
        flipped = ((group_ids + parity) % 2 == 1)[:, None, None]
        trailing = jnp.where(flipped, anti_part[:, 1], sym_part[:, 1])
        sources = jnp.stack([leading, trailing], axis=1)
        return jnp.einsum("gspk,gsfp->gkf", masked, sources, preferred_element_type=F32)

    partials = jnp.stack([half_term(0), half_term(1)], axis=1)
    return lax.psum_scatter(
        partials.astype(BF16), "lat", scatter_dimension=2, tiled=True
    ).astype(F32)


def fused_kernel(
    lat_n,
    ma_n,
    assign_ref,
    window_ref,
    four_hbm,
    leg_hbm,
    out_hbm,
    out_ref,
    four_ref,
    leg_ref,
    stage,
    recv,
    weight,
    part,
    landed,
    send_sem,
    recv_sem,
    psend_sem,
    precv_sem,
    leg_sem,
    four_sem,
    out_sem,
):
    groups_here = leg_ref.shape[0]
    fields_here = four_ref.shape[2]
    rows = four_ref.shape[3]
    pair = rows // 2
    body = pair // 128 * 128
    tail = pair - body
    kcols = leg_ref.shape[3]
    block = kcols // lat_n
    hemi = lat_n // 2
    half_ma = ma_n // 2
    half_f = half_ma * fields_here

    lat = lax.axis_index("lat")
    ma = lax.axis_index("ma")
    side = lat // hemi
    mine = side
    partner = lax.rem(lat + hemi, lat_n)
    my_half = ma // half_ma

    rows_copy = pltpu.make_async_copy(four_hbm, four_ref, four_sem)
    rows_copy.start()
    table_copy = pltpu.make_async_copy(leg_hbm, leg_ref, leg_sem)
    table_copy.start()

    barrier = pltpu.get_barrier_semaphore()
    met = 0
    for r in range(ma_n):
        there = lax.rem(ma + r, ma_n)
        if r:
            pl.semaphore_signal(barrier, inc=1, device_id=(lat, there), device_id_type=MESH)
            met += 1
        pl.semaphore_signal(barrier, inc=1, device_id=(partner, there), device_id_type=MESH)
        met += 1
    for r in range(1, lat_n):
        if r != hemi:
            pl.semaphore_signal(
                barrier, inc=1, device_id=(lax.rem(lat + r, lat_n), ma), device_id_type=MESH
            )
            met += 1

    def pack(q, g):
        slab = four_ref.at[assign_ref[q * groups_here + g]]
        for t in range(2):
            a = slab[0, :, t * pair : (t + 1) * pair]
            b = slab[1, :, t * pair : (t + 1) * pair]
            stage[g, q, t] = jnp.concatenate(
                [a[:, :body], b[:, :body], a[:, body:], b[:, body:]], axis=1
            )

    def row_copy(g, q, own):
        t = mine if own else 1 - mine
        return pltpu.make_async_remote_copy(
            src_ref=stage.at[g, q, t],
            dst_ref=recv.at[g, side, ma],
            send_sem=send_sem.at[g, q, t],
            recv_sem=recv_sem.at[g, side, ma],
            device_id=(lat if own else partner, q),
            device_id_type=MESH,
        )

    def pack_send(g):
        def step(r, c):
            hop = r // 2
            half = lax.rem(my_half + 1 + r, 2)
            q = half * half_ma + lax.rem(ma + hop, half_ma)
            pack(q, g)
            row_copy(g, q, False).start()

            @pl.when(q != ma)
            def _():
                row_copy(g, q, True).start()

            return c

        lax.fori_loop(0, ma_n, step, 0)
        pltpu.make_async_copy(
            stage.at[g, ma, mine], recv.at[g, side, ma], recv_sem.at[g, side, ma]
        ).start()

    rows_copy.wait()
    pl.semaphore_wait(barrier, met)
    for g in range(groups_here):
        pack_send(g)
    table_copy.wait()

    ids = [window_ref[assign_ref[ma * groups_here + g]] for g in range(groups_here)]
    for g in range(groups_here):
        for e in range(2):

            def fill(j, c, g=g, e=e):
                start = pl.multiple_of(j * 128, 128)
                table = leg_ref[g, :, e, pl.ds(start, 128)].astype(F32).T
                k = start + lax.broadcasted_iota(jnp.int32, (128, 1), 0)
                low = 2 * k + e < 2 * kcols - ids[g]
                lower = jnp.where(low, table, 0.0)
                upper = jnp.where(low, 0.0, table)
                weight[g, e, pl.ds(start, 128), :] = jnp.concatenate(
                    [lower[:, :body], upper[:, :body], lower[:, body:], upper[:, body:]],
                    axis=1,
                ).astype(BF16)
                return c

            lax.fori_loop(0, kcols // 128, fill, 0)

    lane = lax.broadcasted_iota(jnp.int32, (1, rows), 1)
    in_upper = ((lane >= body) & (lane < 2 * body)) | (lane >= 2 * body + tail)

    def part_copy(g, h, e, r):
        there = lax.rem(lat + r, lat_n)
        return pltpu.make_async_remote_copy(
            src_ref=part.at[g, h, there, e],
            dst_ref=landed.at[r - 1, g, h, e],
            send_sem=psend_sem.at[r - 1, g, h, e],
            recv_sem=precv_sem.at[r - 1, g, h, e],
            device_id=(there, ma),
            device_id_type=MESH,
        )

    def multiply(g, h):
        def arrive(m, c):
            for ns in range(2):
                piece = recv.at[g, ns, h * half_ma + m]
                pltpu.make_async_copy(piece, piece, recv_sem.at[g, ns, h * half_ma + m]).wait()
            return c

        lax.fori_loop(0, half_ma, arrive, 0)
        north = recv[g, 0, pl.ds(h * half_ma, half_ma)].reshape(half_f, rows).astype(F32)
        south = recv[g, 1, pl.ds(h * half_ma, half_ma)].reshape(half_f, rows).astype(F32)
        for e in range(2):
            odd = lax.rem(ids[g] + e, 2).astype(F32)
            sign = jnp.where(in_upper, 1.0 - 2.0 * odd, 1.0 - 2.0 * e)
            source = (north + sign * south).astype(BF16)
            for r in (*range(1, lat_n), 0):
                d = lax.rem(lat + r, lat_n)
                part[g, h, d, e] = lax.dot_general(
                    weight[g, e, pl.ds(pl.multiple_of(d * block, 16), block), :],
                    source,
                    (((1,), (1,)), ((), ())),
                    preferred_element_type=F32,
                ).astype(BF16)
                if r:
                    part_copy(g, h, e, r).start()

    def out_copy(g, h, e):
        at = pl.multiple_of(h * half_f, 128)
        return pltpu.make_async_copy(
            out_ref.at[g, e, h], out_hbm.at[g, e, :, pl.ds(at, half_f)], out_sem.at[g, e, h]
        )

    def finish(g, h):
        for e in range(2):
            for r in range(1, lat_n):
                part_copy(g, h, e, r).wait_recv()
            total = part[g, h, lat, e].astype(F32)
            for r in range(1, lat_n):
                total = total + landed[r - 1, g, h, e].astype(F32)
            out_ref[g, e, h] = total
            out_copy(g, h, e).start()

    chunks = [(g, (my_half + j) % 2) for g in range(groups_here) for j in range(2)]
    for i, (g, h) in enumerate(chunks):
        multiply(g, h)
        if i:
            finish(*chunks[i - 1])
    finish(*chunks[-1])

    for g in range(groups_here):

        def sent(q, c, g=g):
            row_copy(g, q, False).wait_send()

            @pl.when(q != ma)
            def _():
                row_copy(g, q, True).wait_send()

            return c

        lax.fori_loop(0, ma_n, sent, 0)
    for g, h in chunks:
        for e in range(2):
            for r in range(1, lat_n):
                part_copy(g, h, e, r).wait_send()
            out_copy(g, h, e).wait()


def fused_on_device(fourier, legendre, window, assign):
    lat_n, ma_n = lax.axis_size("lat"), lax.axis_size("ma")
    _, slots, fields_here, rows = fourier.shape
    groups_here, pair, parities, kcols = legendre.shape
    block = kcols // lat_n
    fields = fields_here * ma_n
    smem = pl.BlockSpec(memory_space=pltpu.SMEM)
    hbm = pl.BlockSpec(memory_space=pltpu.HBM)
    dma = pltpu.SemaphoreType.DMA
    return pl.pallas_call(
        functools.partial(fused_kernel, lat_n, ma_n),
        out_shape=jax.ShapeDtypeStruct((groups_here, 2, block, fields), F32),
        in_specs=[smem, smem, hbm, hbm],
        out_specs=hbm,
        scratch_shapes=[
            pltpu.VMEM((groups_here, 2, 2, block, fields // 2), F32),
            pltpu.VMEM(fourier.shape, BF16),
            pltpu.VMEM(legendre.shape, BF16),
            pltpu.VMEM((groups_here, ma_n, 2, fields_here, rows), BF16),
            pltpu.VMEM((groups_here, 2, ma_n, fields_here, rows), BF16),
            pltpu.VMEM((groups_here, 2, kcols, rows), BF16),
            pltpu.VMEM((groups_here, 2, lat_n, 2, block, fields // 2), BF16),
            pltpu.VMEM((lat_n - 1, groups_here, 2, 2, block, fields // 2), BF16),
            dma((groups_here, ma_n, 2)),
            dma((groups_here, 2, ma_n)),
            dma((lat_n - 1, groups_here, 2, 2)),
            dma((lat_n - 1, groups_here, 2, 2)),
            dma,
            dma,
            dma((groups_here, 2, 2)),
        ],
        compiler_params=pltpu.CompilerParams(
            collective_id=0, has_side_effects=True, vmem_limit_bytes=63 * 2**20
        ),
        cost_estimate=pl.CostEstimate(
            flops=8 * groups_here * kcols * rows * fields,
            bytes_accessed=2 * (fourier.size + legendre.size),
            transcendentals=0,
        ),
    )(assign, window, fourier, legendre)


def fits_kernel(mesh, fourier, legendre):
    lat_n, ma_n = mesh.shape["lat"], mesh.shape["ma"]
    fields_here = fourier.shape[2] // ma_n
    pair = legendre.shape[1] // lat_n
    block = legendre.shape[3] // lat_n
    return (
        fourier.shape[1] == 2
        and lat_n == 4
        and ma_n == 8
        and fields_here % 16 == 0
        and (fields_here * ma_n) % 256 == 0
        and (2 * pair) % 128 == 0
        and block % 16 == 0
        and legendre.shape[3] % 128 == 0
    )


def solution(mesh):
    def run(fourier, legendre, window, assign):
        fused = fits_kernel(mesh, fourier, legendre)
        return jax.shard_map(
            fused_on_device if fused else plain_on_device,
            mesh=mesh,
            in_specs=(P(None, None, "ma", "lat"), P("ma", "lat", None, None), P(), P()),
            out_specs=P("ma", None, "lat", None),
            check_vma=False,
        )(fourier, legendre, window, assign)

    return run
```
